128 devices in a mesh: mu: 16 (over y, z), aux: 8 (over x, core).
Axes of the slice: x: 4, y: 4, z: 4, core: 2. Of those that a mesh axis runs over, the one named last changes fastest.
Arguments:
- blocks: bfloat16 [512, 192, 4096], P('mu', 'aux'), may hold values from -0.75 to 0.75
- row_block_of_slot: int32 [512], P('mu'), may hold values from 0 to 7
- column_block_of_slot: int32 [512], P('mu'), may hold values from 0 to 127
- block_count: int32 [16], P('mu'), may hold values from 8 to 32, as said below
- occupied: bfloat16 [8192, 64], replicated, may hold values from -6 to 6
Outputs:
- exchange: float32 [8192, 8192], P('mu', 'aux')
The draws below stay inside these ranges and needn't reach their ends.
Inputs may be any that keep to these rules, and one draw needn't show every extreme that they name: `block_count`: some index of mu has all 32 slots live.
All inputs are finite; a program needn't handle non-finite values.
Results may differ from the reference program's by a relative error of at most 0.0022.
Values may be sent and summed in bfloat16 or wider, within the bound.
No kernel may reach another device: no remote copies, remote signals or barrier semaphores. Data moves between devices by JAX's collectives and lax.ppermute only.
A program may use at most 128 MiB of HBM per device.

```python
import jax
import jax.numpy as jnp
from jax import lax

BLOCK_WIDTH = 64
OCC = 64
MB_DEV = 8
SLOT_COUNT = 32
NB = 128
NBF = 8192
AUX_FUNCTIONS = 192
SLOTS = 512
N_MU = 16


def draw_block_count(key, part):
    key = jax.random.fold_in(key, 11)
    leading_index, second = jax.random.split(key)
    slot_counts = jax.random.randint(leading_index, (N_MU,), max(1, SLOT_COUNT // 4), SLOT_COUNT + 1)
    target_positions = jax.random.randint(second, (), 0, N_MU)
    return slot_counts.at[target_positions].set(SLOT_COUNT).astype(jnp.int32)


def place_ends(entries, rng, smallest, largest):
    longest = entries.shape.index(max(entries.shape))
    spots = []
    for shift in (0, 1):
        where = [jax.random.randint(jax.random.fold_in(rng, axis), (), 0, length) for axis, length in enumerate(entries.shape)]
        where[longest] = (where[longest] + shift) % entries.shape[longest]
        spots.append(tuple(where))
    return entries.at[spots[0]].set(smallest).at[spots[1]].set(largest)


def level_of(stream_key, dims, cuts, least, top_value):
    def one(dim, parts):
        heights = jax.random.uniform(jax.random.fold_in(jax.random.fold_in(stream_key, 6), dim), (parts,), jnp.float32, least / len(cuts), top_value / len(cuts))
        return jnp.repeat(jnp.exp(heights), dims[dim] // parts).reshape((-1,) + (1,) * (len(dims) - dim - 1))

    factor_of = one(*cuts[0])
    for cut in cuts[1:]:
        factor_of = factor_of * one(*cut)
    return factor_of


def gaussian(key, dims, spread, most, cuts=(), held_as=jnp.bfloat16):
    drawn = jax.random.normal(key, dims, jnp.float32) * spread
    if len(cuts) > 0:
        drawn = level_of(key, dims, cuts, -0.22, 0.18) * drawn
    return jnp.clip(drawn, min=-most, max=most).astype(held_as)


def setup_inputs(seed: int = 0) -> dict:
    key_of = jax.random.split(jax.random.key(seed), 6)
    blocks = gaussian(key_of[0], (SLOTS, AUX_FUNCTIONS, BLOCK_WIDTH * BLOCK_WIDTH), BLOCK_WIDTH ** -0.5, 0.75, ((0, 16), (1, 8)))
    row_block_of_slot = place_ends(jax.random.randint(key_of[1], (SLOTS,), 0, MB_DEV), jax.random.fold_in(key_of[1], 1), 0, MB_DEV - 1).astype(jnp.int32)
    column_block_of_slot = place_ends(jax.random.randint(key_of[2], (SLOTS,), 0, NB), jax.random.fold_in(key_of[2], 1), 0, NB - 1).astype(jnp.int32)
    block_count = draw_block_count(jax.random.fold_in(key_of[5], 71), 0)
    occupied = gaussian(key_of[4], (NBF, OCC), 1.0, 6.0)
    return {"blocks": blocks, "row_block_of_slot": row_block_of_slot, "column_block_of_slot": column_block_of_slot, "block_count": block_count, "occupied": occupied}


def device_rows(block_tiles, row_indices, column_indices, count, occupied):
    slot_offsets = jnp.arange(SLOT_COUNT, dtype=jnp.int32)
    live = slot_offsets < count
    block_tiles = jnp.where(live[:, None, None, None], block_tiles, jnp.zeros_like(block_tiles))
    coeff = occupied.reshape(NB, BLOCK_WIDTH, OCC)[column_indices]
    prods = jnp.einsum('spab,sbi->spai', block_tiles.astype(jnp.float32), coeff.astype(jnp.float32), precision=lax.Precision.HIGHEST)
    onehot = (row_indices[None, :] == jnp.arange(MB_DEV, dtype=jnp.int32)[:, None]).astype(jnp.float32)
    summed = jnp.einsum('ms,spai->mapi', onehot, prods, precision=lax.Precision.HIGHEST)
    return summed.reshape(MB_DEV * BLOCK_WIDTH, AUX_FUNCTIONS * OCC).astype(jnp.bfloat16)

def reference(blocks, row_block_of_slot, column_block_of_slot, block_count, occupied):
    block_tiles = blocks.reshape(N_MU, SLOT_COUNT, AUX_FUNCTIONS, BLOCK_WIDTH, BLOCK_WIDTH)
    row_indices = row_block_of_slot.reshape(N_MU, SLOT_COUNT)
    column_indices = column_block_of_slot.reshape(N_MU, SLOT_COUNT)

    def one(index):
        return device_rows(block_tiles[index], row_indices[index], column_indices[index], block_count[index], occupied)
    half = lax.map(one, jnp.arange(N_MU, dtype=jnp.int32)).reshape(NBF, AUX_FUNCTIONS * OCC)
    product = jnp.dot(half, half.T, preferred_element_type=jnp.float32)
    return product / jnp.sqrt(jnp.float32(AUX_FUNCTIONS * OCC))
```

```python
import jax
import jax.numpy as jnp
from jax import lax
from jax.experimental import pallas as pl
from jax.experimental.pallas import tpu as pltpu
from jax.sharding import PartitionSpec as P

W = 64
CHUNKS = (512,)
AXES = ("mu", "aux")
VMEM = 56 * 1024 * 1024


def device_index(y, z, x, c):
    return ((y % 4) * 4 + z % 4) * 8 + (x % 4) * 2 + c % 2


def permute(a, move):
    pairs = []
    for y in range(4):
        for z in range(4):
            for x in range(4):
                for c in range(2):
                    pairs.append((device_index(y, z, x, c), device_index(*move(y, z, x, c))))
    return lax.ppermute(a, AXES, pairs)


def strips(k):
    o, r = sum(CHUNKS[:k]), CHUNKS[k]
    out, at = [], 0
    for j in range((o + r) // 128):
        out.append((o, r, j * 128, at))
        at += r
    for j in range(r // 128 if o else 0):
        out.append((0, o, o + j * 128, at))
        at += o
    return out, at


def half_kernel(rows_ref, cols_ref, count_ref, blocks_ref, occ_ref, *refs):
    outs, (acc, turn) = refs[: len(CHUNKS)], refs[len(CHUNKS):]
    step = pl.program_id(0)
    per, naux, wide = blocks_ref.shape
    tiles = wide // 128

    @pl.when(step == 0)
    def _():
        acc[...] = jnp.zeros_like(acc)

    lane = lax.broadcasted_iota(jnp.int32, (W, 128), 1)

    @pl.loop(0, per)
    def _(j):
        s = step * per + j

        @pl.when(s < count_ref[0])
        def _():
            col = cols_ref[s]
            pair = occ_ref[:, pl.ds(pl.multiple_of(lax.shift_right_logical(col, 1) * 128, 128), 128)]
            pair = pair.astype(jnp.float32)
            other = pltpu.roll(pair, 64, 1)
            odd = (col & 1) == 1
            left = jnp.where(odd, other, pair)
            right = jnp.where(odd, pair, other)
            coeff = jnp.concatenate(
                [jnp.where(lane < 64, left, 0.0), jnp.where(lane < 64, 0.0, right)], axis=0
            ).astype(jnp.bfloat16)
            x = blocks_ref[j].astype(jnp.float32)
            x = jnp.concatenate([x[:, t * 128:(t + 1) * 128] for t in range(tiles)], axis=0)
            prod = lax.dot_general(
                x.astype(jnp.bfloat16), coeff, (((1,), (1,)), ((), ())), preferred_element_type=jnp.float32
            )
            acc[rows_ref[s]] += prod

    @pl.when(step == pl.num_programs(0) - 1)
    def _():
        low = lax.broadcasted_iota(jnp.int32, (tiles, 128), 1) < 64
        at = 0
        for k, r in enumerate(CHUNKS):
            for b in range(r // W):
                m = at // W + b
                for q in range(naux // 2):
                    even = acc[m, pl.ds(2 * q, tiles, stride=naux), :]
                    odd = acc[m, pl.ds(2 * q + 1, tiles, stride=naux), :]
                    turn[pl.ds(0, tiles, stride=2), :] = jnp.where(low, even, pltpu.roll(odd, 64, 1))
                    turn[pl.ds(1, tiles, stride=2), :] = jnp.where(low, pltpu.roll(even, 64, 1), odd)
                    outs[k][b * W:(b + 1) * W, q * 128:(q + 1) * 128] = turn[...].astype(jnp.bfloat16)
            at += r


def half_rows(blocks, rows, cols, count, occ_t):
    slots, naux, wide = blocks.shape
    per = slots // 4
    wide_out = naux * W
    return pl.pallas_call(
        half_kernel,
        grid_spec=pltpu.PrefetchScalarGridSpec(
            num_scalar_prefetch=3,
            grid=(slots // per,),
            in_specs=[
                pl.BlockSpec((per, naux, wide), lambda i, *_: (i, 0, 0)),
                pl.BlockSpec(occ_t.shape, lambda i, *_: (0, 0)),
            ],
            out_specs=[pl.BlockSpec((r, wide_out), lambda i, *_: (0, 0)) for r in CHUNKS],
            scratch_shapes=[
                pltpu.VMEM((8, naux * wide // 128, 128), jnp.float32),
                pltpu.VMEM((W, 128), jnp.float32),
            ],
        ),
        out_shape=[jax.ShapeDtypeStruct((r, wide_out), jnp.bfloat16) for r in CHUNKS],
        compiler_params=pltpu.CompilerParams(vmem_limit_bytes=VMEM),
        cost_estimate=pl.CostEstimate(flops=2 * 10**9, bytes_accessed=8 * 10**6, transcendentals=0),
        name="half_rows",
    )(rows, cols, count, blocks, occ_t)


def product_kernel(k, place_ref, *refs):
    pieces = [4 if r is None else r for r in ()]
    n = (k + 1) * 5
    i_refs, j_refs = refs[:n], refs[n:2 * n]
    mine, theirs = refs[2 * n], refs[2 * n + 1]
    iv, jv, ob, in_sem, out_sem = refs[2 * n + 2:]
    core, y = place_ref[0], place_ref[1]
    o, r = sum(CHUNKS[:k]), CHUNKS[k]
    copies = []
    for side, (srcs, dst) in enumerate(((i_refs, iv), (j_refs, jv))):
        at = 0
        for m in range(k + 1):
            h = CHUNKS[m]
            own, plus, minus, two_a, two_b = srcs[5 * m:5 * m + 5]
            for src, where in (
                (own, dst.at[0, pl.ds(at, h)]),
                (plus, dst.at[1, pl.ds(at, h)]),
                (minus, dst.at[3, pl.ds(at, h)]),
                (two_a, dst.at[2, pl.ds(at, h // 2)]),
                (two_b, dst.at[2, pl.ds(at + h // 2, h // 2)]),
            ):
                copy = pltpu.make_async_copy(src, where, in_sem.at[side, len(copies) % n])
                copy.start()
                copies.append(copy)
            at += h
    for copy in copies:
        copy.wait()
    plan, _ = strips(k)

    @pl.loop(0, 16)
    def _(t):
        dz, dy = lax.shift_right_logical(t, 2), t & 3
        nt = (((1,), (1,)), ((), ()))
        first = lax.dot_general(
            iv[dz, o:o + r, :], jv[dy, 0:o + r, :], nt, preferred_element_type=jnp.float32
        )
        for (row, rows, col, at) in plan:
            if row == o:
                ob[dz, dy, at:at + rows, :] = first[:, col:col + 128]
        if o:
            second = lax.dot_general(
                iv[dz, 0:o, :], jv[dy, o:o + r, :], nt, preferred_element_type=jnp.float32
            )
            for (row, rows, col, at) in plan:
                if row != o:
                    ob[dz, dy, at:at + rows, :] = second[:, col - o:col - o + 128]
        target = (y + dy) & 3
        e = dz & 1

        @pl.when(lax.shift_right_logical(dz, 1) == core)
        def _():
            pltpu.make_async_copy(ob.at[dz, dy], mine.at[target, e], out_sem.at[dz, dy]).start()

        @pl.when(lax.shift_right_logical(dz, 1) != core)
        def _():
            pltpu.make_async_copy(ob.at[dz, dy], theirs.at[target, e], out_sem.at[dz, dy]).start()

    @pl.loop(0, 16)
    def _(t):
        dz, dy = lax.shift_right_logical(t, 2), t & 3
        pltpu.make_async_copy(ob.at[dz, dy], mine.at[0, 0], out_sem.at[dz, dy]).wait()


def product(k, place, i_pieces, j_pieces):
    _, size = strips(k)
    upto = sum(CHUNKS[:k + 1])
    depth = i_pieces[0].shape[1]
    n = (k + 1) * 5
    shape = jax.ShapeDtypeStruct((4, 2, size, 128), jnp.float32)
    return pl.pallas_call(
        lambda *refs: product_kernel(k, *refs),
        grid_spec=pltpu.PrefetchScalarGridSpec(
            num_scalar_prefetch=1,
            grid=(1,),
            in_specs=[pl.BlockSpec(memory_space=pl.ANY)] * (2 * n),
            out_specs=[pl.BlockSpec(memory_space=pl.ANY)] * 2,
            scratch_shapes=[
                pltpu.VMEM((4, upto, depth), jnp.bfloat16),
                pltpu.VMEM((4, upto, depth), jnp.bfloat16),
                pltpu.VMEM((4, 4, size, 128), jnp.float32),
                pltpu.SemaphoreType.DMA((2, n)),
                pltpu.SemaphoreType.DMA((4, 4)),
            ],
        ),
        out_shape=[shape, shape],
        compiler_params=pltpu.CompilerParams(vmem_limit_bytes=VMEM),
        cost_estimate=pl.CostEstimate(
            flops=2 * 16 * size * 128 * depth, bytes_accessed=16 * size * 512 + 16 * upto * depth, transcendentals=0
        ),
        name="product",
    )(place, *i_pieces, *j_pieces)


def core_kernel(place_ref, mine, other, rounded, own):
    total = mine[...] + other[...]
    rounded[...] = total.astype(jnp.bfloat16)

    @pl.when(pl.program_id(0) == place_ref[2])
    def _():
        own[...] = total[0]


def core_sum(place, mine, other):
    _, two, size, _ = mine.shape
    block = pl.BlockSpec((1, two, size, 128), lambda i, *_: (i, 0, 0, 0))
    return pl.pallas_call(
        core_kernel,
        grid_spec=pltpu.PrefetchScalarGridSpec(
            num_scalar_prefetch=1,
            grid=(4,),
            in_specs=[block, block],
            out_specs=[block, pl.BlockSpec((two, size, 128), lambda i, *_: (0, 0, 0))],
        ),
        out_shape=[
            jax.ShapeDtypeStruct(mine.shape, jnp.bfloat16),
            jax.ShapeDtypeStruct(mine.shape[1:], jnp.float32),
        ],
        compiler_params=pltpu.CompilerParams(vmem_limit_bytes=VMEM),
        cost_estimate=pl.CostEstimate(flops=mine.size, bytes_accessed=11 * mine.size, transcendentals=0),
        name="core_sum",
    )(place, mine, other)


def aux_kernel(place_ref, scale_ref, parts, own, first, second):
    x = place_ref[2]
    for e, out in ((0, first), (1, second)):
        total = own[e]
        for j in range(1, 4):
            total = total + parts[(x + j) & 3, e].astype(jnp.float32)
        out[...] = total * scale_ref[0]


def aux_sum(place, scale, parts, own):
    _, two, size, _ = parts.shape
    steps = 4
    part = size // steps
    shape = jax.ShapeDtypeStruct((size, 128), jnp.float32)
    return pl.pallas_call(
        aux_kernel,
        grid_spec=pltpu.PrefetchScalarGridSpec(
            num_scalar_prefetch=2,
            grid=(steps,),
            in_specs=[
                pl.BlockSpec((4, two, part, 128), lambda i, *_: (0, 0, i, 0)),
                pl.BlockSpec((two, part, 128), lambda i, *_: (0, i, 0)),
            ],
            out_specs=[pl.BlockSpec((part, 128), lambda i, *_: (i, 0))] * 2,
        ),
        out_shape=[shape, shape],
        compiler_params=pltpu.CompilerParams(vmem_limit_bytes=VMEM),
        cost_estimate=pl.CostEstimate(flops=parts.size, bytes_accessed=5 * parts.size, transcendentals=0),
        name="aux_sum",
    )(place, scale, parts, own)


def place_kernel(place_ref, *refs):
    out = refs[-1]
    half = place_ref[3]
    for k in range(len(CHUNKS)):
        for n in range(2):
            base = (half if n == 0 else 1 - half) * 512
            for (row, rows, col, at) in strips(k)[0]:
                out[row:row + rows, pl.ds(pl.multiple_of(base + col, 128), 128)] = refs[2 * k + n][at:at + rows, :]


def assemble(place, pieces):
    return pl.pallas_call(
        place_kernel,
        grid_spec=pltpu.PrefetchScalarGridSpec(
            num_scalar_prefetch=1,
            grid=(1,),
            in_specs=[pl.BlockSpec(p.shape, lambda i, *_: (0, 0)) for p in pieces],
            out_specs=pl.BlockSpec((512, 1024), lambda i, *_: (0, 0)),
        ),
        out_shape=jax.ShapeDtypeStruct((512, 1024), jnp.float32),
        compiler_params=pltpu.CompilerParams(vmem_limit_bytes=VMEM),
        name="assemble",
    )(place, *pieces)


def gather(h, plus, minus):
    half = h.shape[0] // 2
    from_below, from_above = permute(h, plus), permute(h, minus)
    two_a = permute(from_below[:half], plus)
    two_b = permute(from_above[half:], minus)
    return [h, from_above, from_below, two_a, two_b]


def body(blocks, row_block_of_slot, column_block_of_slot, block_count, occupied):
    mu, aux = lax.axis_index("mu"), lax.axis_index("aux")
    y, z, x, c = mu // 4, mu % 4, aux // 2, aux % 2
    place = jnp.stack([c, y, x, z % 2]).astype(jnp.int32)
    total_aux = blocks.shape[1] * lax.axis_size("aux") * occupied.shape[1]
    scale = (1.0 / jnp.sqrt(jnp.float32(total_aux))).reshape(1)
    halves = half_rows(blocks, row_block_of_slot, column_block_of_slot, block_count, occupied.T)
    i_pieces, j_pieces, done = [], [], []
    groups = [[2 * g + core for g in range(4)] for core in range(2)]
    for k, h in enumerate(halves):
        i_pieces += gather(h, lambda y, z, x, c: (y, z + 1, x, c), lambda y, z, x, c: (y, z - 1, x, c))
        j_pieces += gather(h, lambda y, z, x, c: (y + 1, z, x, c), lambda y, z, x, c: (y - 1, z, x, c))
        mine, theirs = product(k, place, list(i_pieces), list(j_pieces))
        other = permute(theirs, lambda y, z, x, c: (y, z, x, 1 - c))
        rounded, own = core_sum(place, mine, other)
        parts = lax.all_to_all(rounded, "aux", 0, 0, tiled=True, axis_index_groups=groups)
        first, second = aux_sum(place, scale, parts, own)
        done.append(permute(first, lambda y, z, x, c: (y, z + 2 * c, x, z // 2)))
        done.append(permute(second, lambda y, z, x, c: (y, z + 2 * c + 1, x, z // 2)))
    return assemble(place, done)


def solution(mesh):
    return jax.shard_map(
        body,
        mesh=mesh,
        in_specs=(P("mu", "aux", None), P("mu"), P("mu"), P("mu"), P()),
        out_specs=P("mu", "aux"),
        check_vma=False,
    )
```

```python
import jax
import jax.numpy as jnp
from jax import lax
from jax.experimental import pallas as pl
from jax.experimental.pallas import tpu as pltpu
from jax.sharding import PartitionSpec as P

W = 64
CHUNKS = (512,)
AXES = ("mu", "aux")
MIB = 1024 * 1024


def device_index(y, z, x, c):
    return ((y % 4) * 4 + z % 4) * 8 + (x % 4) * 2 + c % 2


def permute(a, move):
    pairs = []
    for y in range(4):
        for z in range(4):
            for x in range(4):
                for c in range(2):
                    pairs.append((device_index(y, z, x, c), device_index(*move(y, z, x, c))))
    return lax.ppermute(a, AXES, pairs)


def column_strips():
    return [(m, j) for m, r in enumerate(CHUNKS) for j in range(0, r // 2, 128)]


def plan(k):
    out, at = [], 0
    for strip, (m, _) in enumerate(column_strips()):
        if m <= k:
            out.append((sum(CHUNKS[:k]), CHUNKS[k], strip, at))
            at += CHUNKS[k]
        if m == k and k:
            rows = sum(CHUNKS[:k])
            out.append((0, rows, strip, at))
            at += rows
    return out, at


def half_kernel(rows_ref, cols_ref, count_ref, place_ref, blocks_ref, occ_ref, *refs):
    outs, (acc, turn) = refs[: len(CHUNKS)], refs[len(CHUNKS):]
    step = pl.program_id(0)
    per, naux, wide = blocks_ref.shape
    tiles = wide // 128

    @pl.when(step == 0)
    def _():
        acc[...] = jnp.zeros_like(acc)

    lane = lax.broadcasted_iota(jnp.int32, (W, 128), 1)

    @pl.loop(0, per, unroll=4)
    def _(j):
        s = step * per + j

        col = cols_ref[s]
        pair = occ_ref[:, pl.ds(pl.multiple_of(lax.shift_right_logical(col, 1) * 128, 128), 128)]
        pair = jnp.where(s < count_ref[0], pair.astype(jnp.float32), 0.0)
        other = pltpu.roll(pair, 64, 1)
        odd = (col & 1) == 1
        left = jnp.where(odd, other, pair)
        right = jnp.where(odd, pair, other)
        coeff = jnp.concatenate(
            [jnp.where(lane < 64, left, 0.0), jnp.where(lane < 64, 0.0, right)], axis=0
        ).astype(jnp.bfloat16)
        x = blocks_ref[j].astype(jnp.float32)
        x = jnp.concatenate([x[:, t * 128:(t + 1) * 128] for t in range(tiles)], axis=0)
        prod = lax.dot_general(
            x.astype(jnp.bfloat16), coeff, (((1,), (1,)), ((), ())), preferred_element_type=jnp.float32
        )
        acc[rows_ref[s]] += prod

    @pl.when(step == pl.num_programs(0) - 1)
    def _():
        core = place_ref[0]
        low = lax.broadcasted_iota(jnp.int32, (tiles, 128), 1) < 64
        at = 0
        for k, r in enumerate(CHUNKS):
            span = r // 2 // W
            for h in range(2):
                base = at // W + (h + core - 2 * h * core) * span
                for b in range(span):
                    m = base + b
                    for q in range(naux // 2):
                        even = acc[m, pl.ds(2 * q, tiles, stride=naux), :]
                        odd = acc[m, pl.ds(2 * q + 1, tiles, stride=naux), :]
                        turn[q, pl.ds(0, tiles, stride=2), :] = jnp.where(low, even, pltpu.roll(odd, 64, 1))
                        turn[q, pl.ds(1, tiles, stride=2), :] = jnp.where(low, pltpu.roll(even, 64, 1), odd)
                        outs[k][h, b * W:(b + 1) * W, q * 128:(q + 1) * 128] = turn[q].astype(jnp.bfloat16)
            at += r


def half_rows(blocks, rows, cols, count, place, occ_t):
    slots, naux, wide = blocks.shape
    per = slots // 4
    depth = naux * W
    return pl.pallas_call(
        half_kernel,
        grid_spec=pltpu.PrefetchScalarGridSpec(
            num_scalar_prefetch=4,
            grid=(slots // per,),
            in_specs=[
                pl.BlockSpec((per, naux, wide), lambda i, *_: (i, 0, 0)),
                pl.BlockSpec(occ_t.shape, lambda i, *_: (0, 0)),
            ],
            out_specs=[pl.BlockSpec((2, r // 2, depth), lambda i, *_: (0, 0, 0)) for r in CHUNKS],
            scratch_shapes=[
                pltpu.VMEM((8, naux * wide // 128, 128), jnp.float32),
                pltpu.VMEM((naux // 2, W, 128), jnp.float32),
            ],
        ),
        out_shape=[jax.ShapeDtypeStruct((2, r // 2, depth), jnp.bfloat16) for r in CHUNKS],
        compiler_params=pltpu.CompilerParams(vmem_limit_bytes=56 * MIB),
        cost_estimate=pl.CostEstimate(flops=2 * 10**9, bytes_accessed=8 * 10**6, transcendentals=0),
        name="half_rows",
    )(rows, cols, count, place, blocks, occ_t)


def product_kernel(k, place_ref, *refs):
    n = k + 1
    i_refs, j_refs = refs[:5 * n], refs[5 * n:9 * n]
    packed, own, iv, jv, ob, fb, i_sem, j_sem, out_sem, own_sem = refs[9 * n:]
    core, y, x, z = place_ref[0], place_ref[1], place_ref[2], place_ref[3]
    depth = i_refs[0].shape[-1]
    o, r = sum(CHUNKS[:k]), CHUNKS[k]

    def start(src, where, sem):
        pltpu.make_async_copy(src, where, sem).start()

    at = 0
    for m in range(n):
        half = CHUNKS[m] // 2
        own_j, near_j, near_other_j, far_j = j_refs[4 * m:4 * m + 4]
        for part in range(2):
            for slot, src in enumerate(
                (own_j.at[0, part], near_j.at[0, part], far_j.at[part], near_other_j.at[1 - part])
            ):
                where = jv.at[pl.ds(4 * at + slot * half, half), pl.ds(part * depth, depth)]
                start(src, where, j_sem)
        at += half
    for slot in range(4):
        at = 0
        for m in range(n):
            half = CHUNKS[m] // 2
            own_i, near_i, near_other_i, far_i, far_other_i = i_refs[5 * m:5 * m + 5]
            first = pl.ds(pl.multiple_of(at + core * half, 64), half)
            second = pl.ds(pl.multiple_of(at + (1 - core) * half, 64), half)
            for part in range(2):
                here, there = pl.ds(part * depth, depth), pl.ds((1 - part) * depth, depth)
                sem = i_sem.at[slot]
                if slot == 0:
                    start(own_i.at[0, part], iv.at[slot, first, here], sem)
                    start(own_i.at[1, part], iv.at[slot, second, here], sem)
                elif slot == 1:
                    start(near_i.at[0, part], iv.at[slot, first, here], sem)
                    start(near_i.at[1, part], iv.at[slot, second, here], sem)
                elif slot == 2:
                    start(far_i.at[part], iv.at[slot, first, here], sem)
                    start(far_other_i.at[part], iv.at[slot, second, there], sem)
                else:
                    start(near_other_i.at[0, part], iv.at[slot, second, there], sem)
                    start(near_other_i.at[1, part], iv.at[slot, first, there], sem)
            at += 2 * half
    pltpu.make_async_copy(jv, jv, j_sem).wait()
    pieces, size = plan(k)
    where_strip = column_strips()

    def moved(slot):
        return jnp.where(slot == 0, 0, jnp.where(slot == 2, 2, (slot - 2) * (2 * core - 1)))

    @pl.loop(0, 4)
    def _(slot):
        pltpu.make_async_copy(iv.at[slot], iv.at[slot], i_sem.at[slot]).wait()
        target = (z + moved(slot)) & 3
        nt = (((1,), (1,)), ((), ()))

        def put(result, first_row, first_col):
            for row, rows, strip, at in pieces:
                if row == first_row:
                    m, j = where_strip[strip]
                    for q in range(4):
                        col = 2 * sum(CHUNKS[:m]) + q * (CHUNKS[m] // 2) + j - first_col
                        tile = result[:, col:col + 128]
                        ob[slot, q, at:at + rows, :] = tile.astype(jnp.bfloat16)

                        @pl.when(jnp.logical_and(slot == 0, ((y + moved(q)) & 3) == x))
                        def _():
                            fb[at:at + rows, :] = tile

        put(lax.dot_general(
            iv[slot, o:o + r, :], jv[...], nt, preferred_element_type=jnp.float32
        ), o, 0)
        if o:
            put(lax.dot_general(
                iv[slot, 0:o, :], jv[2 * o:, :], nt, preferred_element_type=jnp.float32
            ), 0, 2 * o)
        for q in range(4):
            to = target * 4 + ((y + moved(q)) & 3)
            start(ob.at[slot, q], packed.at[to], out_sem.at[slot, q])

        @pl.when(slot == 0)
        def _():
            start(fb, own, own_sem)

    pltpu.make_async_copy(fb, own, own_sem).wait()
    for q in range(4):
        for slot in range(4):
            pltpu.make_async_copy(ob.at[slot, q], packed.at[0], out_sem.at[slot, q]).wait()


def product(k, place, i_pieces, j_pieces):
    _, size = plan(k)
    upto = sum(CHUNKS[:k + 1])
    depth = i_pieces[0].shape[-1]
    return pl.pallas_call(
        lambda *refs: product_kernel(k, *refs),
        grid_spec=pltpu.PrefetchScalarGridSpec(
            num_scalar_prefetch=1,
            grid=(1,),
            in_specs=[pl.BlockSpec(memory_space=pl.ANY)] * (len(i_pieces) + len(j_pieces)),
            out_specs=[pl.BlockSpec(memory_space=pl.ANY)] * 2,
            scratch_shapes=[
                pltpu.VMEM((4, upto, 2 * depth), jnp.bfloat16),
                pltpu.VMEM((2 * upto, 2 * depth), jnp.bfloat16),
                pltpu.VMEM((4, 4, size, 128), jnp.bfloat16),
                pltpu.VMEM((size, 128), jnp.float32),
                pltpu.SemaphoreType.DMA((4,)),
                pltpu.SemaphoreType.DMA,
                pltpu.SemaphoreType.DMA((4, 4)),
                pltpu.SemaphoreType.DMA,
            ],
        ),
        out_shape=[
            jax.ShapeDtypeStruct((16, size, 128), jnp.bfloat16),
            jax.ShapeDtypeStruct((size, 128), jnp.float32),
        ],
        compiler_params=pltpu.CompilerParams(vmem_limit_bytes=56 * MIB),
        cost_estimate=pl.CostEstimate(
            flops=2 * 16 * size * 128 * 2 * depth, bytes_accessed=24 * upto * depth, transcendentals=0
        ),
        name="product",
    )(place, *i_pieces, *j_pieces)


def aux_kernel(place_ref, scale_ref, parts, own, keep, give):
    core, x, z = place_ref[0], place_ref[2], place_ref[3]
    for out, side in ((keep, core), (give, 1 - core)):
        for n in range(2):
            source = 2 * side + n
            total = jnp.where(source == z, own[...], parts[4 * source + x].astype(jnp.float32))
            for j in range(1, 4):
                total = total + parts[4 * source + ((x + j) & 3)].astype(jnp.float32)
            out[n] = total * scale_ref[0]


def aux_sum(place, scale, parts, own):
    _, size, _ = parts.shape
    steps = 4
    part = size // steps
    shape = jax.ShapeDtypeStruct((2, size, 128), jnp.float32)
    return pl.pallas_call(
        aux_kernel,
        grid_spec=pltpu.PrefetchScalarGridSpec(
            num_scalar_prefetch=2,
            grid=(steps,),
            in_specs=[
                pl.BlockSpec((16, part, 128), lambda i, *_: (0, i, 0)),
                pl.BlockSpec((part, 128), lambda i, *_: (i, 0)),
            ],
            out_specs=[pl.BlockSpec((2, part, 128), lambda i, *_: (0, i, 0))] * 2,
        ),
        out_shape=[shape, shape],
        compiler_params=pltpu.CompilerParams(vmem_limit_bytes=24 * MIB),
        cost_estimate=pl.CostEstimate(flops=parts.size, bytes_accessed=5 * parts.size, transcendentals=0),
        name="aux_sum",
    )(place, scale, parts, own)


def place_kernel(steps, place_ref, *refs):
    pieces, out, sem = refs[:2 * len(steps)], refs[-2], refs[-1]
    core = place_ref[0]
    copies = []
    for i, k in enumerate(steps):
        for src, half in ((pieces[2 * i], core), (pieces[2 * i + 1], 1 - core)):
            for row, rows, strip, at in plan(k)[0]:
                m, j = column_strips()[strip]
                for n in range(2):
                    base = n * 512 + sum(CHUNKS[:m]) + half * (CHUNKS[m] // 2) + j
                    copy = pltpu.make_async_copy(
                        src.at[n, pl.ds(at, rows)],
                        out.at[pl.ds(row, rows), pl.ds(pl.multiple_of(base, 128), 128)],
                        sem.at[len(copies)],
                    )
                    copy.start()
                    copies.append(copy)
    for copy in copies:
        copy.wait()


def assemble(place, steps, pieces, before):
    count = sum(4 * len(plan(k)[0]) for k in steps)
    ins = list(pieces) + ([before] if before is not None else [])
    return pl.pallas_call(
        lambda *refs: place_kernel(steps, *refs),
        grid_spec=pltpu.PrefetchScalarGridSpec(
            num_scalar_prefetch=1,
            grid=(1,),
            in_specs=[pl.BlockSpec(memory_space=pl.ANY)] * len(ins),
            out_specs=pl.BlockSpec(memory_space=pl.ANY),
            scratch_shapes=[pltpu.SemaphoreType.DMA((count,))],
        ),
        out_shape=jax.ShapeDtypeStruct((512, 1024), jnp.float32),
        input_output_aliases={len(ins): 0} if before is not None else {},
        compiler_params=pltpu.CompilerParams(vmem_limit_bytes=16 * MIB),
        name="assemble",
    )(place, *ins)


def along_z(y, z, x, c):
    return (y, z - 1 + 2 * c, x, c)


def along_y(y, z, x, c):
    return (y - 1 + 2 * c, z, x, c)


def other_core(y, z, x, c):
    return (y, z, x, 1 - c)


def body(blocks, row_block_of_slot, column_block_of_slot, block_count, occupied):
    mu, aux = lax.axis_index("mu"), lax.axis_index("aux")
    place = jnp.stack([aux & 1, mu >> 2, aux >> 1, mu & 3]).astype(jnp.int32)
    total_aux = blocks.shape[1] * lax.axis_size("aux") * occupied.shape[1]
    scale = (1.0 / jnp.sqrt(jnp.float32(total_aux))).reshape(1)
    halves = half_rows(blocks, row_block_of_slot, column_block_of_slot, block_count, place, occupied.T)
    i_pieces, j_pieces, done = [], [], []
    groups = [
        [device_index(y, z, x, c) for z in range(4) for x in range(4)] for y in range(4) for c in range(2)
    ]
    for k, h in enumerate(halves):
        sibling = permute(h, other_core)
        h = jnp.stack([h, sibling[::-1]], axis=1)
        z_near, y_near = permute(h, along_z), permute(h, along_y)
        z_far, y_far = permute(z_near[0], along_z), permute(y_near[0], along_y)
        i_pieces += [h, z_near, permute(z_near, other_core), z_far, permute(z_far, other_core)]
        j_pieces += [h, y_near, permute(y_near[1], other_core), y_far]
        ready = lax.optimization_barrier((place, parts))[0] if k else place
        packed, own = product(k, ready, list(i_pieces), list(j_pieces))
        parts = lax.all_to_all(packed, AXES, 0, 0, tiled=True, axis_index_groups=groups)
        keep, give = aux_sum(place, scale, parts, own)
        done += [keep, permute(give, other_core)]
    last = len(CHUNKS) - 1
    out = assemble(place, range(last), done[:2 * last], None) if last else None
    return assemble(place, [last], done[2 * last:], out)


def solution(mesh):
    return jax.shard_map(
        body,
        mesh=mesh,
        in_specs=(P("mu", "aux", None), P("mu"), P("mu"), P("mu"), P()),
        out_specs=P("mu", "aux"),
        check_vma=False,
    )
```

```python
import jax
import jax.numpy as jnp
from jax import lax
from jax.experimental import pallas as pl
from jax.experimental.pallas import tpu as pltpu
from jax.sharding import PartitionSpec as P

W = 64
ROWS = 512
HALF = ROWS // 2
AXES = ("mu", "aux")
MIB = 1024 * 1024


def device_index(y, z, x, c):
    return ((y % 4) * 4 + z % 4) * 8 + (x % 4) * 2 + c % 2


def permute(a, move):
    pairs = []
    for y in range(4):
        for z in range(4):
            for x in range(4):
                for c in range(2):
                    pairs.append((device_index(y, z, x, c), device_index(*move(y, z, x, c))))
    return lax.ppermute(a, AXES, pairs)


def half_kernel(rows_ref, cols_ref, count_ref, blocks_ref, occ_ref, out, acc, turn):
    step = pl.program_id(0)
    per, naux, wide = blocks_ref.shape
    tiles = wide // 128

    @pl.when(step == 0)
    def _():
        acc[...] = jnp.zeros_like(acc)

    lane = lax.broadcasted_iota(jnp.int32, (W, 128), 1)

    @pl.loop(0, per, unroll=8)
    def _(j):
        s = step * per + j

        col = cols_ref[s]
        pair = occ_ref[:, pl.ds(pl.multiple_of(lax.shift_right_logical(col, 1) * 128, 128), 128)]
        pair = jnp.where(s < count_ref[0], pair.astype(jnp.float32), 0.0)
        other = pltpu.roll(pair, 64, 1)
        odd = (col & 1) == 1
        left = jnp.where(odd, other, pair)
        right = jnp.where(odd, pair, other)
        coeff = jnp.concatenate(
            [jnp.where(lane < 64, left, 0.0), jnp.where(lane < 64, 0.0, right)], axis=0
        ).astype(jnp.bfloat16)
        x = blocks_ref[j].astype(jnp.float32)
        x = jnp.concatenate([x[:, t * 128:(t + 1) * 128] for t in range(tiles)], axis=0)
        prod = lax.dot_general(
            x.astype(jnp.bfloat16), coeff, (((1,), (1,)), ((), ())), preferred_element_type=jnp.float32
        )
        acc[rows_ref[s]] += prod

    @pl.when(step == pl.num_programs(0) - 1)
    def _():
        core = lax.axis_index("aux") & 1
        low = lax.broadcasted_iota(jnp.int32, (tiles, 128), 1) < 64
        span = HALF // W
        for h in range(2):
            base = (h + core - 2 * h * core) * span
            for b in range(span):
                m = base + b
                for q in range(naux // 2):
                    even = acc[m, pl.ds(2 * q, tiles, stride=naux), :]
                    odd = acc[m, pl.ds(2 * q + 1, tiles, stride=naux), :]
                    turn[q, pl.ds(0, tiles, stride=2), :] = jnp.where(low, even, pltpu.roll(odd, 64, 1))
                    turn[q, pl.ds(1, tiles, stride=2), :] = jnp.where(low, pltpu.roll(even, 64, 1), odd)
                    out[h, b * W:(b + 1) * W, q * 128:(q + 1) * 128] = turn[q].astype(jnp.bfloat16)


def half_rows(blocks, rows, cols, count, occ_t):
    slots, naux, wide = blocks.shape
    per = slots // 4
    depth = naux * W
    return pl.pallas_call(
        half_kernel,
        grid_spec=pltpu.PrefetchScalarGridSpec(
            num_scalar_prefetch=3,
            grid=(slots // per,),
            in_specs=[
                pl.BlockSpec((per, naux, wide), lambda i, *_: (i, 0, 0)),
                pl.BlockSpec(occ_t.shape, lambda i, *_: (0, 0)),
            ],
            out_specs=pl.BlockSpec((2, HALF, depth), lambda i, *_: (0, 0, 0)),
            scratch_shapes=[
                pltpu.VMEM((8, naux * wide // 128, 128), jnp.float32),
                pltpu.VMEM((naux // 2, W, 128), jnp.float32),
            ],
        ),
        out_shape=jax.ShapeDtypeStruct((2, HALF, depth), jnp.bfloat16),
        compiler_params=pltpu.CompilerParams(vmem_limit_bytes=56 * MIB),
        cost_estimate=pl.CostEstimate(flops=2 * 10**9, bytes_accessed=8 * 10**6, transcendentals=0),
        name="half_rows",
    )(rows, cols, count, blocks, occ_t)


STRIPS = HALF // 128


def moved(slot, core):
    return jnp.where(slot == 0, 0, jnp.where(slot == 3, 2, (2 * slot - 3) * (2 * core - 1)))


def product_kernel(late, place_ref, *refs):
    units, slots = (8, 4) if late else (5, 3)
    rows, refs = refs[:units], refs[units:]
    columns, refs = refs[:slots], refs[slots:]
    packed, iv, jv, ob, i_sem, j_sem, out_sem = refs[1 if late else 0:]
    core, y, z = place_ref[0], place_ref[1], place_ref[3]
    depth = rows[0].shape[-1]
    lanes = (pl.ds(0, depth), pl.ds(depth, depth))

    def start(src, where, sem):
        pltpu.make_async_copy(src, where, sem).start()

    def load_rows(unit):
        for p in range(2):
            start(rows[unit].at[p], iv.at[unit, :, lanes[1 - p if unit in (3, 5, 7) else p]], i_sem.at[unit])

    def load_columns(q):
        for p in range(2):
            start(columns[q].at[p], jv.at[pl.ds(q * HALF, HALF), lanes[1 - p if q == 2 else p]], j_sem)

    def wait_rows(unit):
        pltpu.make_async_copy(iv.at[unit], iv.at[unit], i_sem.at[unit]).wait()

    def multiply(unit, first, last):
        result = lax.dot_general(
            iv[unit], jv[first * HALF:last * HALF, :], (((1,), (1,)), ((), ())), preferred_element_type=jnp.float32
        )
        slot = jnp.where(unit < 2, 0, jnp.where(unit >= 6, 3, jnp.where(unit % 2 == 1, 2, 1)))
        mine = jnp.logical_or(unit == 0, jnp.logical_or(unit == 2, jnp.logical_or(unit == 5, unit == 6)))
        span = pl.ds(pl.multiple_of(jnp.where(mine, core, 1 - core) * HALF, HALF), HALF)
        row = ((z + moved(slot, core)) & 3) * 4
        for q in range(first, last):
            for j in range(STRIPS):
                col = (q - first) * HALF + j * 128
                ob[unit, q, j] = result[:, col:col + 128].astype(jnp.bfloat16)
            to = row + ((y + moved(q, core)) & 3)
            start(ob.at[unit, q], packed.at[to, :, span], out_sem.at[unit])

    def finish(unit, first, last):
        whole = ob.at[unit, pl.ds(first, last - first)]
        pltpu.make_async_copy(whole, whole, out_sem.at[unit]).wait()

    for q in range(slots):
        load_columns(q)
    if late:
        for unit in (5, 6, 7, 0, 1, 2, 3, 4):
            load_rows(unit)
    else:
        for unit in range(5):
            load_rows(unit)
    pltpu.make_async_copy(jv, jv, j_sem).wait()

    if late:
        @pl.loop(5, 8)
        def _(unit):
            wait_rows(unit)
            multiply(unit, 0, 4)

    @pl.loop(0, 5)
    def _(unit):
        wait_rows(unit)
        multiply(unit, *((3, 4) if late else (0, 3)))

    if late:
        @pl.loop(5, 8)
        def _(unit):
            finish(unit, 0, 4)

    @pl.loop(0, 5)
    def _(unit):
        finish(unit, *((3, 4) if late else (0, 3)))


def product(late, place, rows, columns, before=()):
    depth = rows[0].shape[-1]
    ins = list(rows) + list(columns) + list(before)
    units, slots = len(rows), len(columns)
    return pl.pallas_call(
        lambda *refs: product_kernel(late, *refs),
        grid_spec=pltpu.PrefetchScalarGridSpec(
            num_scalar_prefetch=1,
            grid=(1,),
            in_specs=[pl.BlockSpec(memory_space=pl.ANY)] * len(ins),
            out_specs=pl.BlockSpec(memory_space=pl.ANY),
            scratch_shapes=[
                pltpu.VMEM((units, HALF, 2 * depth), jnp.bfloat16),
                pltpu.VMEM((slots * HALF, 2 * depth), jnp.bfloat16),
                pltpu.VMEM((units, slots, STRIPS, HALF, 128), jnp.bfloat16),
                pltpu.SemaphoreType.DMA((units,)),
                pltpu.SemaphoreType.DMA,
                pltpu.SemaphoreType.DMA((units,)),
            ],
        ),
        out_shape=jax.ShapeDtypeStruct((16, STRIPS, ROWS, 128), jnp.bfloat16),
        input_output_aliases={len(ins): 0} if late else {},
        compiler_params=pltpu.CompilerParams(vmem_limit_bytes=(30 if late else 20) * MIB),
        cost_estimate=pl.CostEstimate(
            flops=(17 if late else 15) * HALF * HALF * 2 * 2 * depth, bytes_accessed=(units + slots) * ROWS * 2 * depth,
            transcendentals=0,
        ),
        name="product_late" if late else "product_early",
    )(place, *ins)


def sum_kernel(keep, place_ref, scale_ref, parts, out):
    core = place_ref[0]
    for n in range(2):
        total = parts[4 * n].astype(jnp.float32)
        for j in range(1, 4):
            total = total + parts[4 * n + j].astype(jnp.float32)
        total = total * scale_ref[0]
        if keep:
            for j in range(STRIPS):
                base = n * ROWS + core * HALF + j * 128
                out[:, pl.ds(pl.multiple_of(base, 128), 128)] = total[j]
        else:
            out[n] = total


def aux_sum(keep, place, scale, parts):
    steps = 4
    rows = ROWS // steps
    if keep:
        out_spec = pl.BlockSpec((rows, 2 * ROWS), lambda i, *_: (i, 0))
        shape = (ROWS, 2 * ROWS)
    else:
        out_spec = pl.BlockSpec((2, STRIPS, rows, 128), lambda i, *_: (0, 0, i, 0))
        shape = (2, STRIPS, ROWS, 128)
    return pl.pallas_call(
        lambda *refs: sum_kernel(keep, *refs),
        grid_spec=pltpu.PrefetchScalarGridSpec(
            num_scalar_prefetch=2,
            grid=(steps,),
            in_specs=[
                pl.BlockSpec(
                    (8, STRIPS, rows, 128), lambda i, place, _: (place[0] if keep else 1 - place[0], 0, i, 0)
                ),
            ],
            out_specs=out_spec,
        ),
        out_shape=jax.ShapeDtypeStruct(shape, jnp.float32),
        compiler_params=pltpu.CompilerParams(vmem_limit_bytes=24 * MIB),
        cost_estimate=pl.CostEstimate(flops=parts.size, bytes_accessed=3 * parts.size, transcendentals=0),
        name="sum_keep" if keep else "sum_give",
    )(place, scale, parts)


def place_kernel(place_ref, src, before, out, sem):
    core = place_ref[0]
    copies = []
    for n in range(2):
        for j in range(HALF // 128):
            base = n * ROWS + (1 - core) * HALF + j * 128
            copies.append(pltpu.make_async_copy(
                src.at[n, j], out.at[:, pl.ds(pl.multiple_of(base, 128), 128)], sem.at[n, j]
            ))
    for copy in copies:
        copy.start()
    for copy in copies:
        copy.wait()


def assemble(place, received, before):
    return pl.pallas_call(
        place_kernel,
        grid_spec=pltpu.PrefetchScalarGridSpec(
            num_scalar_prefetch=1,
            grid=(1,),
            in_specs=[pl.BlockSpec(memory_space=pl.ANY)] * 2,
            out_specs=pl.BlockSpec(memory_space=pl.ANY),
            scratch_shapes=[pltpu.SemaphoreType.DMA((2, HALF // 128))],
        ),
        out_shape=jax.ShapeDtypeStruct((ROWS, 2 * ROWS), jnp.float32),
        input_output_aliases={2: 0},
        compiler_params=pltpu.CompilerParams(vmem_limit_bytes=16 * MIB),
        name="assemble",
    )(place, received, before)


def along_z(y, z, x, c):
    return (y, z - 1 + 2 * c, x, c)


def along_y(y, z, x, c):
    return (y - 1 + 2 * c, z, x, c)


def across_y(y, z, x, c):
    return (y - 1 + 2 * c, z, x, 1 - c)


def other_core(y, z, x, c):
    return (y, z, x, 1 - c)


def body(blocks, row_block_of_slot, column_block_of_slot, block_count, occupied):
    mu, aux = lax.axis_index("mu"), lax.axis_index("aux")
    place = jnp.stack([aux & 1, mu >> 2, aux >> 1, mu & 3]).astype(jnp.int32)
    total_aux = blocks.shape[1] * lax.axis_size("aux") * occupied.shape[1]
    scale = (1.0 / jnp.sqrt(jnp.float32(total_aux))).reshape(1)
    groups = [
        [device_index(y, z, x, c) for z in range(4) for x in range(4)] for y in range(4) for c in range(2)
    ]
    h = half_rows(blocks, row_block_of_slot, column_block_of_slot, block_count, occupied.T)
    sibling = permute(h, other_core)
    own = [jnp.stack([h[0], sibling[1]]), jnp.stack([h[1], sibling[0]])]
    z_near = [permute(a, along_z) for a in own]
    y_near, y_other = permute(own[0], along_y), permute(own[1], across_y)
    z_far, y_far = permute(z_near[0], along_z), permute(y_near, along_y)
    z_other = [permute(a, other_core) for a in z_near]
    rows, columns = own + [z_near[0], z_other[0], z_near[1]], [own[0], y_near, y_other]
    early = product(False, place, rows, columns)
    z_far, y_far, early = lax.optimization_barrier((z_far, y_far, early))
    rows, columns = rows + [z_other[1], z_far, permute(z_far, other_core)], columns + [y_far]
    packed = product(True, place, rows, columns, [early])
    parts = lax.all_to_all(packed, AXES, 0, 0, tiled=True, axis_index_groups=groups)
    give = aux_sum(False, place, scale, parts)
    received = permute(give, other_core)
    return assemble(place, received, aux_sum(True, place, scale, parts))


def solution(mesh):
    return jax.shard_map(
        body,
        mesh=mesh,
        in_specs=(P("mu", "aux", None), P("mu"), P("mu"), P("mu"), P()),
        out_specs=P("mu", "aux"),
        check_vma=False,
    )
```

```python
import jax
import jax.numpy as jnp
from jax import lax
from jax.experimental import pallas as pl
from jax.experimental.pallas import tpu as pltpu
from jax.sharding import PartitionSpec as P

W = 64
ROWS = 512
HALF = ROWS // 2
AXES = ("mu", "aux")
MIB = 1024 * 1024


def device_index(y, z, x, c):
    return ((y % 4) * 4 + z % 4) * 8 + (x % 4) * 2 + c % 2


def permute(a, move):
    pairs = []
    for y in range(4):
        for z in range(4):
            for x in range(4):
                for c in range(2):
                    pairs.append((device_index(y, z, x, c), device_index(*move(y, z, x, c))))
    return lax.ppermute(a, AXES, pairs)


def half_kernel(rows_ref, cols_ref, count_ref, blocks_ref, occ_ref, out, acc, turn):
    step = pl.program_id(0)
    per, naux, wide = blocks_ref.shape
    tiles = wide // 128

    @pl.when(step == 0)
    def _():
        acc[...] = jnp.zeros_like(acc)

    lane = lax.broadcasted_iota(jnp.int32, (W, 128), 1)

    @pl.loop(0, per, unroll=8)
    def _(j):
        s = step * per + j

        col = cols_ref[s]
        pair = occ_ref[:, pl.ds(pl.multiple_of(lax.shift_right_logical(col, 1) * 128, 128), 128)]
        pair = jnp.where(s < count_ref[0], pair.astype(jnp.float32), 0.0)
        other = pltpu.roll(pair, 64, 1)
        odd = (col & 1) == 1
        left = jnp.where(odd, other, pair)
        right = jnp.where(odd, pair, other)
        coeff = jnp.concatenate(
            [jnp.where(lane < 64, left, 0.0), jnp.where(lane < 64, 0.0, right)], axis=0
        ).astype(jnp.bfloat16)
        x = blocks_ref[j].astype(jnp.float32)
        x = jnp.concatenate([x[:, t * 128:(t + 1) * 128] for t in range(tiles)], axis=0)
        prod = lax.dot_general(
            x.astype(jnp.bfloat16), coeff, (((1,), (1,)), ((), ())), preferred_element_type=jnp.float32
        )
        acc[rows_ref[s]] += prod

    @pl.when(step == pl.num_programs(0) - 1)
    def _():
        core = lax.axis_index("aux") & 1
        low = lax.broadcasted_iota(jnp.int32, (tiles, 128), 1) < 64
        span = HALF // W
        for h in range(2):
            base = (h + core - 2 * h * core) * span
            for b in range(span):
                m = base + b
                for q in range(naux // 2):
                    even = acc[m, pl.ds(2 * q, tiles, stride=naux), :]
                    odd = acc[m, pl.ds(2 * q + 1, tiles, stride=naux), :]
                    turn[q, pl.ds(0, tiles, stride=2), :] = jnp.where(low, even, pltpu.roll(odd, 64, 1))
                    turn[q, pl.ds(1, tiles, stride=2), :] = jnp.where(low, pltpu.roll(even, 64, 1), odd)
                    out[h, b * W:(b + 1) * W, q * 128:(q + 1) * 128] = turn[q].astype(jnp.bfloat16)


def half_rows(blocks, rows, cols, count, occ_t):
    slots, naux, wide = blocks.shape
    per = slots // 4
    depth = naux * W
    return pl.pallas_call(
        half_kernel,
        grid_spec=pltpu.PrefetchScalarGridSpec(
            num_scalar_prefetch=3,
            grid=(slots // per,),
            in_specs=[
                pl.BlockSpec((per, naux, wide), lambda i, *_: (i, 0, 0)),
                pl.BlockSpec(occ_t.shape, lambda i, *_: (0, 0)),
            ],
            out_specs=pl.BlockSpec((2, HALF, depth), lambda i, *_: (0, 0, 0)),
            scratch_shapes=[
                pltpu.VMEM((8, naux * wide // 128, 128), jnp.float32),
                pltpu.VMEM((naux // 2, W, 128), jnp.float32),
            ],
        ),
        out_shape=jax.ShapeDtypeStruct((2, HALF, depth), jnp.bfloat16),
        compiler_params=pltpu.CompilerParams(vmem_limit_bytes=56 * MIB),
        cost_estimate=pl.CostEstimate(flops=2 * 10**9, bytes_accessed=8 * 10**6, transcendentals=0),
        name="half_rows",
    )(rows, cols, count, blocks, occ_t)


STRIPS = HALF // 128


def moved(slot, core):
    return jnp.where(slot == 0, 0, jnp.where(slot == 3, 2, (2 * slot - 3) * (2 * core - 1)))


def product_kernel(late, place_ref, *refs):
    units, slots = (8, 4) if late else (5, 3)
    rows, refs = refs[:units], refs[units:]
    columns, refs = refs[:slots], refs[slots:]
    packed, iv, jv, ob, i_sem, j_sem, out_sem = refs[1 if late else 0:]
    core, y, z = place_ref[0], place_ref[1], place_ref[3]
    depth = rows[0].shape[-1]
    lanes = (pl.ds(0, depth), pl.ds(depth, depth))

    def start(src, where, sem):
        pltpu.make_async_copy(src, where, sem).start()

    def load_rows(unit):
        for p in range(2):
            start(rows[unit].at[p], iv.at[unit, :, lanes[1 - p if unit in (3, 5, 7) else p]], i_sem.at[unit])

    def load_columns(q):
        for p in range(2):
            start(columns[q].at[p], jv.at[pl.ds(q * HALF, HALF), lanes[1 - p if q == 2 else p]], j_sem.at[q // 3])

    def wait_rows(unit):
        pltpu.make_async_copy(iv.at[unit], iv.at[unit], i_sem.at[unit]).wait()

    def multiply(unit, first, last):
        result = lax.dot_general(
            iv[unit], jv[first * HALF:last * HALF, :], (((1,), (1,)), ((), ())), preferred_element_type=jnp.float32
        )
        slot = jnp.where(unit < 2, 0, jnp.where(unit >= 6, 3, jnp.where(unit % 2 == 1, 2, 1)))
        mine = jnp.logical_or(unit == 0, jnp.logical_or(unit == 2, jnp.logical_or(unit == 5, unit == 6)))
        span = pl.ds(pl.multiple_of(jnp.where(mine, core, 1 - core) * HALF, HALF), HALF)
        row = ((z + moved(slot, core)) & 3) * 4
        for q in range(first, last):
            for j in range(STRIPS):
                col = (q - first) * HALF + j * 128
                ob[unit, q, j] = result[:, col:col + 128].astype(jnp.bfloat16)
            to = row + ((y + moved(q, core)) & 3)
            start(ob.at[unit, q], packed.at[to, :, span], out_sem.at[unit])

    def finish(unit, first, last):
        whole = ob.at[unit, pl.ds(first, last - first)]
        pltpu.make_async_copy(whole, whole, out_sem.at[unit]).wait()

    def wait_columns(first, last):
        ref = jv.at[pl.ds(first * HALF, (last - first) * HALF)]
        pltpu.make_async_copy(ref, ref, j_sem.at[first // 3]).wait()

    if late:
        load_columns(3)
        load_rows(0)
        load_rows(1)
        wait_columns(3, 4)
        for unit in (2, 3, 4):
            load_rows(unit)
        for q in range(3):
            load_columns(q)
        for unit in (5, 6, 7):
            load_rows(unit)
    else:
        for q in range(3):
            load_columns(q)
        for unit in range(5):
            load_rows(unit)
        wait_columns(0, 3)

    @pl.loop(0, 5)
    def _(unit):
        wait_rows(unit)
        multiply(unit, *((3, 4) if late else (0, 3)))

    if late:
        wait_columns(0, 3)

        @pl.loop(5, 8)
        def _(unit):
            wait_rows(unit)
            multiply(unit, 0, 4)

    if late:
        @pl.loop(5, 8)
        def _(unit):
            finish(unit, 0, 4)

    @pl.loop(0, 5)
    def _(unit):
        finish(unit, *((3, 4) if late else (0, 3)))


def product(late, place, rows, columns, before=()):
    depth = rows[0].shape[-1]
    ins = list(rows) + list(columns) + list(before)
    units, slots = len(rows), len(columns)
    return pl.pallas_call(
        lambda *refs: product_kernel(late, *refs),
        grid_spec=pltpu.PrefetchScalarGridSpec(
            num_scalar_prefetch=1,
            grid=(1,),
            in_specs=[pl.BlockSpec(memory_space=pl.ANY)] * len(ins),
            out_specs=pl.BlockSpec(memory_space=pl.ANY),
            scratch_shapes=[
                pltpu.VMEM((units, HALF, 2 * depth), jnp.bfloat16),
                pltpu.VMEM((slots * HALF, 2 * depth), jnp.bfloat16),
                pltpu.VMEM((units, slots, STRIPS, HALF, 128), jnp.bfloat16),
                pltpu.SemaphoreType.DMA((units,)),
                pltpu.SemaphoreType.DMA((2,)),
                pltpu.SemaphoreType.DMA((units,)),
            ],
        ),
        out_shape=jax.ShapeDtypeStruct((16, STRIPS, ROWS, 128), jnp.bfloat16),
        input_output_aliases={len(ins): 0} if late else {},
        compiler_params=pltpu.CompilerParams(vmem_limit_bytes=(28 if late else 18) * MIB),
        cost_estimate=pl.CostEstimate(
            flops=(17 if late else 15) * HALF * HALF * 2 * 2 * depth, bytes_accessed=(units + slots) * ROWS * 2 * depth,
            transcendentals=0,
        ),
        name="product_late" if late else "product_early",
    )(place, *ins)


def total_of(scale_ref, parts, n):
    total = parts[4 * n].astype(jnp.float32)
    for j in range(1, 4):
        total = total + parts[4 * n + j].astype(jnp.float32)
    return total * scale_ref[0]


def give_kernel(place_ref, scale_ref, parts, out):
    for n in range(2):
        out[n] = total_of(scale_ref, parts, n)


def keep_kernel(place_ref, scale_ref, parts, out, held, sem):
    core, step, steps = place_ref[0], pl.program_id(0), pl.num_programs(0)
    rows = parts.shape[2]

    def copy(i, n, j):
        base = pl.multiple_of(n * ROWS + core * HALF + j * 128, 128)
        where = out.at[pl.ds(pl.multiple_of(i * rows, 128), rows), pl.ds(base, 128)]
        return pltpu.make_async_copy(held.at[i, n, j], where, sem.at[i, n, j])

    for n in range(2):
        held[step, n] = total_of(scale_ref, parts, n)
        for j in range(STRIPS):
            copy(step, n, j).start()

    @pl.when(step == steps - 1)
    def _():
        @pl.loop(0, steps)
        def _(i):
            for n in range(2):
                for j in range(STRIPS):
                    copy(i, n, j).wait()


def aux_sum(keep, place, scale, parts):
    steps = 4
    rows = ROWS // steps
    if keep:
        out_spec = pl.BlockSpec(memory_space=pl.ANY)
        shape = (ROWS, 2 * ROWS)
        scratch = [
            pltpu.VMEM((steps, 2, STRIPS, rows, 128), jnp.float32),
            pltpu.SemaphoreType.DMA((steps, 2, STRIPS)),
        ]
    else:
        out_spec = pl.BlockSpec((2, STRIPS, rows, 128), lambda i, *_: (0, 0, i, 0))
        shape = (2, STRIPS, ROWS, 128)
        scratch = []
    return pl.pallas_call(
        keep_kernel if keep else give_kernel,
        grid_spec=pltpu.PrefetchScalarGridSpec(
            num_scalar_prefetch=2,
            grid=(steps,),
            in_specs=[
                pl.BlockSpec(
                    (8, STRIPS, rows, 128), lambda i, place, _: (place[0] if keep else 1 - place[0], 0, i, 0)
                ),
            ],
            out_specs=out_spec,
            scratch_shapes=scratch,
        ),
        out_shape=jax.ShapeDtypeStruct(shape, jnp.float32),
        compiler_params=pltpu.CompilerParams(vmem_limit_bytes=24 * MIB),
        cost_estimate=pl.CostEstimate(flops=parts.size, bytes_accessed=3 * parts.size, transcendentals=0),
        name="sum_keep" if keep else "sum_give",
    )(place, scale, parts)


def place_kernel(place_ref, src, before, out, sem):
    core = place_ref[0]
    copies = []
    for n in range(2):
        for j in range(STRIPS):
            base = pl.multiple_of(n * ROWS + (1 - core) * HALF + j * 128, 128)
            for i in range(4):
                rows = pl.ds(i * (ROWS // 4), ROWS // 4)
                copies.append(pltpu.make_async_copy(
                    src.at[n, j, rows], out.at[rows, pl.ds(base, 128)], sem.at[n, j, i]
                ))
    for copy in copies:
        copy.start()
    for copy in copies:
        copy.wait()


def assemble(place, received, before):
    return pl.pallas_call(
        place_kernel,
        grid_spec=pltpu.PrefetchScalarGridSpec(
            num_scalar_prefetch=1,
            grid=(1,),
            in_specs=[pl.BlockSpec(memory_space=pl.ANY)] * 2,
            out_specs=pl.BlockSpec(memory_space=pl.ANY),
            scratch_shapes=[pltpu.SemaphoreType.DMA((2, STRIPS, 4))],
        ),
        out_shape=jax.ShapeDtypeStruct((ROWS, 2 * ROWS), jnp.float32),
        input_output_aliases={2: 0},
        compiler_params=pltpu.CompilerParams(vmem_limit_bytes=16 * MIB),
        name="assemble",
    )(place, received, before)


def along_z(y, z, x, c):
    return (y, z - 1 + 2 * c, x, c)


def along_y(y, z, x, c):
    return (y - 1 + 2 * c, z, x, c)


def across_y(y, z, x, c):
    return (y - 1 + 2 * c, z, x, 1 - c)


def other_core(y, z, x, c):
    return (y, z, x, 1 - c)


def body(blocks, row_block_of_slot, column_block_of_slot, block_count, occupied):
    mu, aux = lax.axis_index("mu"), lax.axis_index("aux")
    place = jnp.stack([aux & 1, mu >> 2, aux >> 1, mu & 3]).astype(jnp.int32)
    total_aux = blocks.shape[1] * lax.axis_size("aux") * occupied.shape[1]
    scale = (1.0 / jnp.sqrt(jnp.float32(total_aux))).reshape(1)
    groups = [
        [device_index(y, z, x, c) for z in range(4) for x in range(4)] for y in range(4) for c in range(2)
    ]
    h = half_rows(blocks, row_block_of_slot, column_block_of_slot, block_count, occupied.T)
    sibling = permute(h, other_core)
    own = [jnp.stack([h[0], sibling[1]]), jnp.stack([h[1], sibling[0]])]
    z_near = [permute(a, along_z) for a in own]
    y_near, y_other = permute(own[0], along_y), permute(own[1], across_y)
    z_far, y_far = permute(z_near[0], along_z), permute(y_near, along_y)
    z_other = [permute(a, other_core) for a in z_near]
    rows, columns = own + [z_near[0], z_other[0], z_near[1]], [own[0], y_near, y_other]
    early = product(False, place, rows, columns)
    z_far, y_far, early = lax.optimization_barrier((z_far, y_far, early))
    rows, columns = rows + [z_other[1], z_far, permute(z_far, other_core)], columns + [y_far]
    packed = product(True, place, rows, columns, [early])
    parts = lax.all_to_all(packed, AXES, 0, 0, tiled=True, axis_index_groups=groups)
    give = aux_sum(False, place, scale, parts)
    received = permute(give, other_core)
    return assemble(place, received, aux_sum(True, place, scale, parts))


def solution(mesh):
    return jax.shard_map(
        body,
        mesh=mesh,
        in_specs=(P("mu", "aux", None), P("mu"), P("mu"), P("mu"), P()),
        out_specs=P("mu", "aux"),
        check_vma=False,
    )
```

```python
import jax
import jax.numpy as jnp
from jax import lax
from jax.experimental import pallas as pl
from jax.experimental.pallas import tpu as pltpu
from jax.sharding import PartitionSpec as P

W = 64
ROWS = 512
HALF = ROWS // 2
AXES = ("mu", "aux")
MIB = 1024 * 1024


def device_index(y, z, x, c):
    return ((y % 4) * 4 + z % 4) * 8 + (x % 4) * 2 + c % 2


def permute(a, move):
    pairs = []
    for y in range(4):
        for z in range(4):
            for x in range(4):
                for c in range(2):
                    pairs.append((device_index(y, z, x, c), device_index(*move(y, z, x, c))))
    return lax.ppermute(a, AXES, pairs)


def half_kernel(rows_ref, cols_ref, count_ref, blocks_ref, occ_ref, out, acc, turn):
    step = pl.program_id(0)
    per, naux, wide = blocks_ref.shape
    tiles = wide // 128

    @pl.when(step == 0)
    def _():
        acc[...] = jnp.zeros_like(acc)

    lane = lax.broadcasted_iota(jnp.int32, (W, 128), 1)

    @pl.loop(0, per, unroll=8)
    def _(j):
        s = step * per + j

        col = cols_ref[s]
        pair = occ_ref[:, pl.ds(pl.multiple_of(lax.shift_right_logical(col, 1) * 128, 128), 128)]
        pair = jnp.where(s < count_ref[0], pair.astype(jnp.float32), 0.0)
        other = pltpu.roll(pair, 64, 1)
        odd = (col & 1) == 1
        left = jnp.where(odd, other, pair)
        right = jnp.where(odd, pair, other)
        coeff = jnp.concatenate(
            [jnp.where(lane < 64, left, 0.0), jnp.where(lane < 64, 0.0, right)], axis=0
        ).astype(jnp.bfloat16)
        x = blocks_ref[j]
        x = jnp.concatenate([x[:, t * 128:(t + 1) * 128] for t in range(tiles)], axis=0)
        prod = lax.dot_general(
            x, coeff, (((1,), (1,)), ((), ())), preferred_element_type=jnp.float32
        )
        acc[rows_ref[s]] += prod

    @pl.when(step == pl.num_programs(0) - 1)
    def _():
        core = lax.axis_index("aux") & 1
        low = lax.broadcasted_iota(jnp.int32, (tiles, 128), 1) < 64
        span = HALF // W
        for h in range(2):
            base = (h + core - 2 * h * core) * span
            for b in range(span):
                m = base + b
                for q in range(naux // 2):
                    even = acc[m, pl.ds(2 * q, tiles, stride=naux), :]
                    odd = acc[m, pl.ds(2 * q + 1, tiles, stride=naux), :]
                    turn[q, pl.ds(0, tiles, stride=2), :] = jnp.where(low, even, pltpu.roll(odd, 64, 1))
                    turn[q, pl.ds(1, tiles, stride=2), :] = jnp.where(low, pltpu.roll(even, 64, 1), odd)
                    out[h, b * W:(b + 1) * W, q * 128:(q + 1) * 128] = turn[q].astype(jnp.bfloat16)


def half_rows(blocks, rows, cols, count, occ_t):
    slots, naux, wide = blocks.shape
    per = slots // 4
    depth = naux * W
    return pl.pallas_call(
        half_kernel,
        grid_spec=pltpu.PrefetchScalarGridSpec(
            num_scalar_prefetch=3,
            grid=(slots // per,),
            in_specs=[
                pl.BlockSpec((per, naux, wide), lambda i, *_: (i, 0, 0)),
                pl.BlockSpec(occ_t.shape, lambda i, *_: (0, 0)),
            ],
            out_specs=pl.BlockSpec((2, HALF, depth), lambda i, *_: (0, 0, 0)),
            scratch_shapes=[
                pltpu.VMEM((8, naux * wide // 128, 128), jnp.float32),
                pltpu.VMEM((naux // 2, W, 128), jnp.float32),
            ],
        ),
        out_shape=jax.ShapeDtypeStruct((2, HALF, depth), jnp.bfloat16),
        compiler_params=pltpu.CompilerParams(vmem_limit_bytes=56 * MIB),
        cost_estimate=pl.CostEstimate(flops=2 * 10**9, bytes_accessed=8 * 10**6, transcendentals=0),
        name="half_rows",
    )(rows, cols, count, blocks, occ_t)


STRIPS = HALF // 128


def moved(slot, core):
    return jnp.where(slot == 0, 0, jnp.where(slot == 3, 2, (2 * slot - 3) * (2 * core - 1)))


def product_kernel(late, place_ref, *refs):
    units, slots = (8, 4) if late else (5, 3)
    rows, refs = refs[:units], refs[units:]
    columns, refs = refs[:slots], refs[slots:]
    packed, iv, jv, ob, i_sem, j_sem, out_sem = refs[1 if late else 0:]
    core, y, z = place_ref[0], place_ref[1], place_ref[3]
    depth = rows[0].shape[-1]
    lanes = (pl.ds(0, depth), pl.ds(depth, depth))

    def start(src, where, sem):
        pltpu.make_async_copy(src, where, sem).start()

    def load_rows(unit):
        for p in range(2):
            start(rows[unit].at[p], iv.at[unit, :, lanes[1 - p if unit in (3, 5, 7) else p]], i_sem.at[unit])

    def load_columns(q):
        for p in range(2):
            start(columns[q].at[p], jv.at[pl.ds(q * HALF, HALF), lanes[1 - p if q == 2 else p]], j_sem.at[q // 3])

    def wait_rows(unit):
        pltpu.make_async_copy(iv.at[unit], iv.at[unit], i_sem.at[unit]).wait()

    def multiply(unit, first, last):
        result = lax.dot_general(
            iv[unit], jv[first * HALF:last * HALF, :], (((1,), (1,)), ((), ())), preferred_element_type=jnp.float32
        )
        slot = jnp.where(unit < 2, 0, jnp.where(unit >= 6, 3, jnp.where(unit % 2 == 1, 2, 1)))
        mine = jnp.logical_or(unit == 0, jnp.logical_or(unit == 2, jnp.logical_or(unit == 5, unit == 6)))
        span = pl.ds(pl.multiple_of(jnp.where(mine, core, 1 - core) * HALF, HALF), HALF)
        row = ((z + moved(slot, core)) & 3) * 4
        for q in range(first, last):
            for j in range(STRIPS):
                col = (q - first) * HALF + j * 128
                ob[unit, q, j] = result[:, col:col + 128].astype(jnp.bfloat16)
            to = row + ((y + moved(q, core)) & 3)
            start(ob.at[unit, q], packed.at[to, :, span], out_sem.at[unit])

    def finish(unit, first, last):
        whole = ob.at[unit, pl.ds(first, last - first)]
        pltpu.make_async_copy(whole, whole, out_sem.at[unit]).wait()

    def wait_columns(first, last):
        ref = jv.at[pl.ds(first * HALF, (last - first) * HALF)]
        pltpu.make_async_copy(ref, ref, j_sem.at[first // 3]).wait()

    if late:
        load_columns(3)
        load_rows(0)
        load_rows(1)
        wait_columns(3, 4)
        for unit in (2, 3, 4):
            load_rows(unit)
        for q in range(3):
            load_columns(q)
        for unit in (5, 6, 7):
            load_rows(unit)
    else:
        for q in range(3):
            load_columns(q)
        for unit in range(5):
            load_rows(unit)
        wait_columns(0, 3)

    @pl.loop(0, 5)
    def _(unit):
        wait_rows(unit)
        multiply(unit, *((3, 4) if late else (0, 3)))

    if late:
        wait_columns(0, 3)

        @pl.loop(5, 8)
        def _(unit):
            wait_rows(unit)
            multiply(unit, 0, 4)

    if late:
        @pl.loop(5, 8)
        def _(unit):
            finish(unit, 0, 4)

    @pl.loop(0, 5)
    def _(unit):
        finish(unit, *((3, 4) if late else (0, 3)))


def product(late, place, rows, columns, before=()):
    depth = rows[0].shape[-1]
    ins = list(rows) + list(columns) + list(before)
    units, slots = len(rows), len(columns)
    return pl.pallas_call(
        lambda *refs: product_kernel(late, *refs),
        grid_spec=pltpu.PrefetchScalarGridSpec(
            num_scalar_prefetch=1,
            grid=(1,),
            in_specs=[pl.BlockSpec(memory_space=pl.ANY)] * len(ins),
            out_specs=pl.BlockSpec(memory_space=pl.ANY),
            scratch_shapes=[
                pltpu.VMEM((units, HALF, 2 * depth), jnp.bfloat16),
                pltpu.VMEM((slots * HALF, 2 * depth), jnp.bfloat16),
                pltpu.VMEM((units, slots, STRIPS, HALF, 128), jnp.bfloat16),
                pltpu.SemaphoreType.DMA((units,)),
                pltpu.SemaphoreType.DMA((2,)),
                pltpu.SemaphoreType.DMA((units,)),
            ],
        ),
        out_shape=jax.ShapeDtypeStruct((16, STRIPS, ROWS, 128), jnp.bfloat16),
        input_output_aliases={len(ins): 0} if late else {},
        compiler_params=pltpu.CompilerParams(vmem_limit_bytes=(28 if late else 18) * MIB),
        cost_estimate=pl.CostEstimate(
            flops=(17 if late else 15) * HALF * HALF * 2 * 2 * depth, bytes_accessed=(units + slots) * ROWS * 2 * depth,
            transcendentals=0,
        ),
        name="product_late" if late else "product_early",
    )(place, *ins)


def total_of(scale_ref, parts, n):
    total = parts[4 * n].astype(jnp.float32)
    for j in range(1, 4):
        total = total + parts[4 * n + j].astype(jnp.float32)
    return total * scale_ref[0]


def give_kernel(place_ref, scale_ref, parts, out):
    for n in range(2):
        out[n] = total_of(scale_ref, parts, n)


def keep_kernel(place_ref, scale_ref, parts, out, held, sem):
    core, step, steps = place_ref[0], pl.program_id(0), pl.num_programs(0)
    rows = parts.shape[2]

    def copy(i, n, j):
        base = pl.multiple_of(n * ROWS + core * HALF + j * 128, 128)
        where = out.at[pl.ds(pl.multiple_of(i * rows, 128), rows), pl.ds(base, 128)]
        return pltpu.make_async_copy(held.at[i, n, j], where, sem.at[i, n, j])

    for n in range(2):
        held[step, n] = total_of(scale_ref, parts, n)
        for j in range(STRIPS):
            copy(step, n, j).start()

    @pl.when(step == steps - 1)
    def _():
        @pl.loop(0, steps)
        def _(i):
            for n in range(2):
                for j in range(STRIPS):
                    copy(i, n, j).wait()


def aux_sum(keep, place, scale, parts):
    steps = 4
    rows = ROWS // steps
    if keep:
        out_spec = pl.BlockSpec(memory_space=pl.ANY)
        shape = (ROWS, 2 * ROWS)
        scratch = [
            pltpu.VMEM((steps, 2, STRIPS, rows, 128), jnp.float32),
            pltpu.SemaphoreType.DMA((steps, 2, STRIPS)),
        ]
    else:
        out_spec = pl.BlockSpec((2, STRIPS, rows, 128), lambda i, *_: (0, 0, i, 0))
        shape = (2, STRIPS, ROWS, 128)
        scratch = []
    return pl.pallas_call(
        keep_kernel if keep else give_kernel,
        grid_spec=pltpu.PrefetchScalarGridSpec(
            num_scalar_prefetch=2,
            grid=(steps,),
            in_specs=[
                pl.BlockSpec(
                    (8, STRIPS, rows, 128), lambda i, place, _: (place[0] if keep else 1 - place[0], 0, i, 0)
                ),
            ],
            out_specs=out_spec,
            scratch_shapes=scratch,
        ),
        out_shape=jax.ShapeDtypeStruct(shape, jnp.float32),
        compiler_params=pltpu.CompilerParams(vmem_limit_bytes=24 * MIB),
        cost_estimate=pl.CostEstimate(flops=parts.size, bytes_accessed=3 * parts.size, transcendentals=0),
        name="sum_keep" if keep else "sum_give",
    )(place, scale, parts)


def place_kernel(place_ref, src, before, out, sem):
    core = place_ref[0]
    copies = []
    for n in range(2):
        for j in range(STRIPS):
            base = pl.multiple_of(n * ROWS + (1 - core) * HALF + j * 128, 128)
            for i in range(4):
                rows = pl.ds(i * (ROWS // 4), ROWS // 4)
                copies.append(pltpu.make_async_copy(
                    src.at[n, j, rows], out.at[rows, pl.ds(base, 128)], sem.at[n, j, i]
                ))
    for copy in copies:
        copy.start()
    for copy in copies:
        copy.wait()


def assemble(place, received, before):
    return pl.pallas_call(
        place_kernel,
        grid_spec=pltpu.PrefetchScalarGridSpec(
            num_scalar_prefetch=1,
            grid=(1,),
            in_specs=[pl.BlockSpec(memory_space=pl.ANY)] * 2,
            out_specs=pl.BlockSpec(memory_space=pl.ANY),
            scratch_shapes=[pltpu.SemaphoreType.DMA((2, STRIPS, 4))],
        ),
        out_shape=jax.ShapeDtypeStruct((ROWS, 2 * ROWS), jnp.float32),
        input_output_aliases={2: 0},
        compiler_params=pltpu.CompilerParams(vmem_limit_bytes=16 * MIB),
        name="assemble",
    )(place, received, before)


def along_z(y, z, x, c):
    return (y, z - 1 + 2 * c, x, c)


def along_y(y, z, x, c):
    return (y - 1 + 2 * c, z, x, c)


def across_y(y, z, x, c):
    return (y - 1 + 2 * c, z, x, 1 - c)


def other_core(y, z, x, c):
    return (y, z, x, 1 - c)


def body(blocks, row_block_of_slot, column_block_of_slot, block_count, occupied):
    mu, aux = lax.axis_index("mu"), lax.axis_index("aux")
    place = jnp.stack([aux & 1, mu >> 2, aux >> 1, mu & 3]).astype(jnp.int32)
    total_aux = blocks.shape[1] * lax.axis_size("aux") * occupied.shape[1]
    scale = (1.0 / jnp.sqrt(jnp.float32(total_aux))).reshape(1)
    groups = [
        [device_index(y, z, x, c) for z in range(4) for x in range(4)] for y in range(4) for c in range(2)
    ]
    h = half_rows(blocks, row_block_of_slot, column_block_of_slot, block_count, occupied.T)
    sibling = permute(h, other_core)
    own = [jnp.stack([h[0], sibling[1]]), jnp.stack([h[1], sibling[0]])]
    z_near = [permute(a, along_z) for a in own]
    y_near, y_other = permute(own[0], along_y), permute(own[1], across_y)
    z_far, y_far = permute(z_near[0], along_z), permute(y_near, along_y)
    z_other = [permute(a, other_core) for a in z_near]
    rows, columns = own + [z_near[0], z_other[0], z_near[1]], [own[0], y_near, y_other]
    early = product(False, place, rows, columns)
    z_far, y_far, early = lax.optimization_barrier((z_far, y_far, early))
    rows, columns = rows + [z_other[1], z_far, permute(z_far, other_core)], columns + [y_far]
    packed = product(True, place, rows, columns, [early])
    parts = lax.all_to_all(packed, AXES, 0, 0, tiled=True, axis_index_groups=groups)
    give = aux_sum(False, place, scale, parts)
    received = permute(give, other_core)
    return assemble(place, received, aux_sum(True, place, scale, parts))


def solution(mesh):
    return jax.shard_map(
        body,
        mesh=mesh,
        in_specs=(P("mu", "aux", None), P("mu"), P("mu"), P("mu"), P()),
        out_specs=P("mu", "aux"),
        check_vma=False,
    )
```

```python
import jax
import jax.numpy as jnp
from jax import lax
from jax.experimental import pallas as pl
from jax.experimental.pallas import tpu as pltpu
from jax.sharding import PartitionSpec as P

W = 64
ROWS = 512
HALF = ROWS // 2
AXES = ("mu", "aux")
MIB = 1024 * 1024


def device_index(y, z, x, c):
    return ((y % 4) * 4 + z % 4) * 8 + (x % 4) * 2 + c % 2


def permute(a, move):
    pairs = []
    for y in range(4):
        for z in range(4):
            for x in range(4):
                for c in range(2):
                    pairs.append((device_index(y, z, x, c), device_index(*move(y, z, x, c))))
    return lax.ppermute(a, AXES, pairs)


def half_kernel(rows_ref, cols_ref, count_ref, blocks_ref, occ_ref, out, acc, turn):
    step = pl.program_id(0)
    per, naux, wide = blocks_ref.shape
    tiles = wide // 128

    @pl.when(step == 0)
    def _():
        acc[...] = jnp.zeros_like(acc)

    lane = lax.broadcasted_iota(jnp.int32, (W, 128), 1)

    @pl.loop(0, per, unroll=8)
    def _(j):
        s = step * per + j

        col = cols_ref[s]
        pair = occ_ref[:, pl.ds(pl.multiple_of(lax.shift_right_logical(col, 1) * 128, 128), 128)]
        pair = jnp.where(s < count_ref[0], pair.astype(jnp.float32), 0.0)
        other = pltpu.roll(pair, 64, 1)
        odd = (col & 1) == 1
        left = jnp.where(odd, other, pair)
        right = jnp.where(odd, pair, other)
        coeff = jnp.concatenate(
            [jnp.where(lane < 64, left, 0.0), jnp.where(lane < 64, 0.0, right)], axis=0
        ).astype(jnp.bfloat16)
        x = blocks_ref[j].astype(jnp.float32)
        x = jnp.concatenate([x[:, t * 128:(t + 1) * 128] for t in range(tiles)], axis=0)
        prod = lax.dot_general(
            x.astype(jnp.bfloat16), coeff, (((1,), (1,)), ((), ())), preferred_element_type=jnp.float32
        )
        acc[rows_ref[s]] += prod

    @pl.when(step == pl.num_programs(0) - 1)
    def _():
        core = lax.axis_index("aux") & 1
        low = lax.broadcasted_iota(jnp.int32, (tiles, 128), 1) < 64
        span = HALF // W
        for h in range(2):
            base = (h + core - 2 * h * core) * span
            for b in range(span):
                m = base + b
                for q in range(naux // 2):
                    even = acc[m, pl.ds(2 * q, tiles, stride=naux), :]
                    odd = acc[m, pl.ds(2 * q + 1, tiles, stride=naux), :]
                    turn[q, pl.ds(0, tiles, stride=2), :] = jnp.where(low, even, pltpu.roll(odd, 64, 1))
                    turn[q, pl.ds(1, tiles, stride=2), :] = jnp.where(low, pltpu.roll(even, 64, 1), odd)
                    out[h, b * W:(b + 1) * W, q * 128:(q + 1) * 128] = turn[q].astype(jnp.bfloat16)


def half_rows(blocks, rows, cols, count, occ_t):
    slots, naux, wide = blocks.shape
    per = slots // 4
    depth = naux * W
    return pl.pallas_call(
        half_kernel,
        grid_spec=pltpu.PrefetchScalarGridSpec(
            num_scalar_prefetch=3,
            grid=(slots // per,),
            in_specs=[
                pl.BlockSpec((per, naux, wide), lambda i, *_: (i, 0, 0)),
                pl.BlockSpec(occ_t.shape, lambda i, *_: (0, 0)),
            ],
            out_specs=pl.BlockSpec((2, HALF, depth), lambda i, *_: (0, 0, 0)),
            scratch_shapes=[
                pltpu.VMEM((8, naux * wide // 128, 128), jnp.float32),
                pltpu.VMEM((naux // 2, W, 128), jnp.float32),
            ],
        ),
        out_shape=jax.ShapeDtypeStruct((2, HALF, depth), jnp.bfloat16),
        compiler_params=pltpu.CompilerParams(vmem_limit_bytes=56 * MIB),
        cost_estimate=pl.CostEstimate(flops=2 * 10**9, bytes_accessed=8 * 10**6, transcendentals=0),
        name="half_rows",
    )(rows, cols, count, blocks, occ_t)


STRIPS = HALF // 128


def moved(slot, core):
    return jnp.where(slot == 0, 0, jnp.where(slot == 3, 2, (2 * slot - 3) * (2 * core - 1)))


def product_kernel(late, place_ref, *refs):
    units, slots = (8, 4) if late else (5, 3)
    rows, refs = refs[:units], refs[units:]
    columns, refs = refs[:slots], refs[slots:]
    packed, iv, jv, ob, i_sem, j_sem, out_sem = refs[1 if late else 0:]
    core, y, z = place_ref[0], place_ref[1], place_ref[3]
    depth = rows[0].shape[-1]
    lanes = (pl.ds(0, depth), pl.ds(depth, depth))

    def start(src, where, sem):
        pltpu.make_async_copy(src, where, sem).start()

    def load_rows(unit):
        for p in range(2):
            start(rows[unit].at[p], iv.at[unit, :, lanes[1 - p if unit in (3, 5, 7) else p]], i_sem.at[unit])

    def load_columns(q):
        for p in range(2):
            start(columns[q].at[p], jv.at[pl.ds(q * HALF, HALF), lanes[1 - p if q == 2 else p]], j_sem.at[q // 3])

    def wait_rows(unit):
        pltpu.make_async_copy(iv.at[unit], iv.at[unit], i_sem.at[unit]).wait()

    def product_of(left, first, last):
        return lax.dot_general(
            left, jv[first * HALF:last * HALF, :], (((1,), (1,)), ((), ())), preferred_element_type=jnp.float32
        )

    def multiply(unit, first, last, result=None):
        if result is None:
            result = product_of(iv[unit], first, last)
        slot = jnp.where(unit < 2, 0, jnp.where(unit >= 6, 3, jnp.where(unit % 2 == 1, 2, 1)))
        mine = jnp.logical_or(unit == 0, jnp.logical_or(unit == 2, jnp.logical_or(unit == 5, unit == 6)))
        span = pl.ds(pl.multiple_of(jnp.where(mine, core, 1 - core) * HALF, HALF), HALF)
        row = ((z + moved(slot, core)) & 3) * 4
        for q in range(first, last):
            for j in range(STRIPS):
                col = (q - first) * HALF + j * 128
                ob[unit, q, j] = result[:, col:col + 128].astype(jnp.bfloat16)
            to = row + ((y + moved(q, core)) & 3)
            start(ob.at[unit, q], packed.at[to, :, span], out_sem.at[unit])

    def finish(unit, first, last):
        whole = ob.at[unit, pl.ds(first, last - first)]
        pltpu.make_async_copy(whole, whole, out_sem.at[unit]).wait()

    def wait_columns(first, last):
        ref = jv.at[pl.ds(first * HALF, (last - first) * HALF)]
        pltpu.make_async_copy(ref, ref, j_sem.at[first // 3]).wait()

    if late:
        load_columns(3)
        load_rows(0)
        load_rows(1)
        wait_columns(3, 4)
        for unit in range(2, 8):
            load_rows(unit)
        for q in range(3):
            load_columns(q)
    else:
        for q in range(3):
            load_columns(q)
        for unit in range(5):
            load_rows(unit)
        wait_columns(0, 3)

    if late:
        @pl.loop(0, 4)
        def _(pair):
            for n in range(2):
                wait_rows(2 * pair + n)
            result = product_of(iv[pl.ds(2 * pair, 2)].reshape(2 * HALF, 2 * depth), 3, 4)
            for n in range(2):
                multiply(2 * pair + n, 3, 4, result[n * HALF:(n + 1) * HALF])

        wait_columns(0, 3)

        @pl.loop(5, 8)
        def _(unit):
            multiply(unit, 0, 3)
    else:
        @pl.loop(0, 5)
        def _(unit):
            wait_rows(unit)
            multiply(unit, 0, 3)

    if late:
        @pl.loop(5, 8)
        def _(unit):
            finish(unit, 0, 4)

    @pl.loop(0, 5)
    def _(unit):
        finish(unit, *((3, 4) if late else (0, 3)))


def product(late, place, rows, columns, before=()):
    depth = rows[0].shape[-1]
    ins = list(rows) + list(columns) + list(before)
    units, slots = len(rows), len(columns)
    return pl.pallas_call(
        lambda *refs: product_kernel(late, *refs),
        grid_spec=pltpu.PrefetchScalarGridSpec(
            num_scalar_prefetch=1,
            grid=(1,),
            in_specs=[pl.BlockSpec(memory_space=pl.ANY)] * len(ins),
            out_specs=pl.BlockSpec(memory_space=pl.ANY),
            scratch_shapes=[
                pltpu.VMEM((units, HALF, 2 * depth), jnp.bfloat16),
                pltpu.VMEM((slots * HALF, 2 * depth), jnp.bfloat16),
                pltpu.VMEM((units, slots, STRIPS, HALF, 128), jnp.bfloat16),
                pltpu.SemaphoreType.DMA((units,)),
                pltpu.SemaphoreType.DMA((2,)),
                pltpu.SemaphoreType.DMA((units,)),
            ],
        ),
        out_shape=jax.ShapeDtypeStruct((16, STRIPS, ROWS, 128), jnp.bfloat16),
        input_output_aliases={len(ins): 0} if late else {},
        compiler_params=pltpu.CompilerParams(vmem_limit_bytes=(28 if late else 18) * MIB),
        cost_estimate=pl.CostEstimate(
            flops=(17 if late else 15) * HALF * HALF * 2 * 2 * depth, bytes_accessed=(units + slots) * ROWS * 2 * depth,
            transcendentals=0,
        ),
        name="product_late" if late else "product_early",
    )(place, *ins)


def total_of(scale_ref, parts, n):
    total = parts[4 * n].astype(jnp.float32)
    for j in range(1, 4):
        total = total + parts[4 * n + j].astype(jnp.float32)
    return total * scale_ref[0]


def give_kernel(place_ref, scale_ref, parts, out):
    for n in range(2):
        out[n] = total_of(scale_ref, parts, n)


def keep_kernel(place_ref, scale_ref, parts, out, held, sem):
    core, step, steps = place_ref[0], pl.program_id(0), pl.num_programs(0)
    rows = parts.shape[2]

    def copy(i, n, j):
        base = pl.multiple_of(n * ROWS + core * HALF + j * 128, 128)
        where = out.at[pl.ds(pl.multiple_of(i * rows, 128), rows), pl.ds(base, 128)]
        return pltpu.make_async_copy(held.at[i, n, j], where, sem.at[i, n, j])

    for n in range(2):
        held[step, n] = total_of(scale_ref, parts, n)
        for j in range(STRIPS):
            copy(step, n, j).start()

    @pl.when(step == steps - 1)
    def _():
        @pl.loop(0, steps)
        def _(i):
            for n in range(2):
                for j in range(STRIPS):
                    copy(i, n, j).wait()


def aux_sum(keep, place, scale, parts):
    steps = 4
    rows = ROWS // steps
    if keep:
        out_spec = pl.BlockSpec(memory_space=pl.ANY)
        shape = (ROWS, 2 * ROWS)
        scratch = [
            pltpu.VMEM((steps, 2, STRIPS, rows, 128), jnp.float32),
            pltpu.SemaphoreType.DMA((steps, 2, STRIPS)),
        ]
    else:
        out_spec = pl.BlockSpec((2, STRIPS, rows, 128), lambda i, *_: (0, 0, i, 0))
        shape = (2, STRIPS, ROWS, 128)
        scratch = []
    return pl.pallas_call(
        keep_kernel if keep else give_kernel,
        grid_spec=pltpu.PrefetchScalarGridSpec(
            num_scalar_prefetch=2,
            grid=(steps,),
            in_specs=[
                pl.BlockSpec(
                    (8, STRIPS, rows, 128), lambda i, place, _: (place[0] if keep else 1 - place[0], 0, i, 0)
                ),
            ],
            out_specs=out_spec,
            scratch_shapes=scratch,
        ),
        out_shape=jax.ShapeDtypeStruct(shape, jnp.float32),
        compiler_params=pltpu.CompilerParams(vmem_limit_bytes=24 * MIB),
        cost_estimate=pl.CostEstimate(flops=parts.size, bytes_accessed=3 * parts.size, transcendentals=0),
        name="sum_keep" if keep else "sum_give",
    )(place, scale, parts)


def place_kernel(place_ref, src, before, out, sem):
    core = place_ref[0]
    copies = []
    for n in range(2):
        for j in range(STRIPS):
            base = pl.multiple_of(n * ROWS + (1 - core) * HALF + j * 128, 128)
            for i in range(4):
                rows = pl.ds(i * (ROWS // 4), ROWS // 4)
                copies.append(pltpu.make_async_copy(
                    src.at[n, j, rows], out.at[rows, pl.ds(base, 128)], sem.at[n, j, i]
                ))
    for copy in copies:
        copy.start()
    for copy in copies:
        copy.wait()


def assemble(place, received, before):
    return pl.pallas_call(
        place_kernel,
        grid_spec=pltpu.PrefetchScalarGridSpec(
            num_scalar_prefetch=1,
            grid=(1,),
            in_specs=[pl.BlockSpec(memory_space=pl.ANY)] * 2,
            out_specs=pl.BlockSpec(memory_space=pl.ANY),
            scratch_shapes=[pltpu.SemaphoreType.DMA((2, STRIPS, 4))],
        ),
        out_shape=jax.ShapeDtypeStruct((ROWS, 2 * ROWS), jnp.float32),
        input_output_aliases={2: 0},
        compiler_params=pltpu.CompilerParams(vmem_limit_bytes=16 * MIB),
        name="assemble",
    )(place, received, before)


def along_z(y, z, x, c):
    return (y, z - 1 + 2 * c, x, c)


def along_y(y, z, x, c):
    return (y - 1 + 2 * c, z, x, c)


def across_y(y, z, x, c):
    return (y - 1 + 2 * c, z, x, 1 - c)


def other_core(y, z, x, c):
    return (y, z, x, 1 - c)


def body(blocks, row_block_of_slot, column_block_of_slot, block_count, occupied):
    mu, aux = lax.axis_index("mu"), lax.axis_index("aux")
    place = jnp.stack([aux & 1, mu >> 2, aux >> 1, mu & 3]).astype(jnp.int32)
    total_aux = blocks.shape[1] * lax.axis_size("aux") * occupied.shape[1]
    scale = (1.0 / jnp.sqrt(jnp.float32(total_aux))).reshape(1)
    groups = [
        [device_index(y, z, x, c) for z in range(4) for x in range(4)] for y in range(4) for c in range(2)
    ]
    h = half_rows(blocks, row_block_of_slot, column_block_of_slot, block_count, occupied.T)
    sibling = permute(h, other_core)
    own = [jnp.stack([h[0], sibling[1]]), jnp.stack([h[1], sibling[0]])]
    z_near = [permute(a, along_z) for a in own]
    y_near, y_other = permute(own[0], along_y), permute(own[1], across_y)
    z_far, y_far = permute(z_near[0], along_z), permute(y_near, along_y)
    z_other = [permute(a, other_core) for a in z_near]
    rows, columns = own + [z_near[0], z_other[0], z_near[1]], [own[0], y_near, y_other]
    early = product(False, place, rows, columns)
    z_far, y_far, early = lax.optimization_barrier((z_far, y_far, early))
    rows, columns = rows + [z_other[1], z_far, permute(z_far, other_core)], columns + [y_far]
    packed = product(True, place, rows, columns, [early])
    parts = lax.all_to_all(packed, AXES, 0, 0, tiled=True, axis_index_groups=groups)
    give = aux_sum(False, place, scale, parts)
    received = permute(give, other_core)
    return assemble(place, received, aux_sum(True, place, scale, parts))


def solution(mesh):
    return jax.shard_map(
        body,
        mesh=mesh,
        in_specs=(P("mu", "aux", None), P("mu"), P("mu"), P("mu"), P()),
        out_specs=P("mu", "aux"),
        check_vma=False,
    )
```
